32 devices in a mesh: gx: 8 (over z, y), gy: 4 (over x, core).
Axes of the slice: x: 2, y: 2, z: 4, core: 2. Of those that a mesh axis runs over, the one named last changes fastest.
Arguments:
- tracer: float32 [1, 24, 128, 512], P(None, None, 'gx', 'gy'), may hold values from -3 to 3
- kappa: float32 [128, 512], P('gx', 'gy'), may hold values from 0.06 to 0.24
- dkappa: float32 [128, 512], P('gx', 'gy'), may hold values from -6 to 6
- precision_weight: float32 [24, 24], replicated, may hold values from -0.08 to 2.08, as said below
- observed: int32 [4, 8, 32], P(None, 'gx', 'gy'), may hold values 0 or 1
Outputs:
- hess_vec: float32 [128, 512], P('gx', 'gy')
- gram: float32 [24, 24], replicated
- curvature: float32 [], replicated
The draws below stay inside these ranges and needn't reach their ends.
Inputs may be any that keep to these rules, and one draw needn't show every extreme that they name: `precision_weight`: symmetric; each diagonal entry exceeds the sum of the magnitudes of the other entries of its row.
All inputs are finite; a program needn't handle non-finite values. No bound on the sum of `observed` on one device may be relied on, other than what follows from the above.
Results may differ from the reference program's by a relative error of at most 0.0001.
Values sent between devices are 32-bit elements; how exact they have to be, the bound alone decides.
A program may use at most 64 MiB of HBM per device.

```python
import math
import jax
import jax.numpy as jnp
from jax import lax

LAYERS = 1
CHANNELS = 24
STEPS = 4
TILE = 16
NX = 128
NY = 512


def draw_tracer(key, part):
    key = jax.random.fold_in(key, 1)
    key_base, key_chan = jax.random.split(key)
    chan_scale = jnp.exp(jax.random.uniform(key_chan, (CHANNELS,), jnp.float32, jnp.log(0.03), jnp.log(0.3)))
    position = jnp.arange(NX).astype(jnp.float32) / (NX - 1)
    shape = (LAYERS, CHANNELS, NX, NY)
    base = jnp.clip(jax.random.normal(key_base, shape, jnp.float32), -5.0, 5.0)
    ramp = jnp.sqrt(1.0 + 2.0 * position)
    return base * chan_scale[None, :, None, None] * ramp[None, None, :, None]


def draw_precision_weight(key, part):
    key = jax.random.fold_in(key, 2)
    raw = jax.random.uniform(key, (CHANNELS, CHANNELS), jnp.float32, -1.0, 1.0)
    return 0.04 * (raw + raw.T) + 2.0 * jnp.eye(CHANNELS, dtype=jnp.float32)


def touch_ends(drawn, own_key, least, high):
    dims = drawn.shape
    spot = [jax.random.randint(jax.random.fold_in(own_key, axis), (), 0, dims[axis]) for axis in range(len(dims))]
    drawn = drawn.at[tuple(spot)].set(least)
    longest = dims.index(max(dims))
    spot[longest] = (spot[longest] + 1) % dims[longest]
    return drawn.at[tuple(spot)].set(high)


def levels(stream_key, shape, cuts, least, high):
    loudness, own = 1.0, jax.random.fold_in(stream_key, 6)
    for dim, shards_of in cuts:
        heights = jnp.exp(jax.random.uniform(jax.random.fold_in(own, dim), (shards_of,), jnp.float32, least / len(cuts), high / len(cuts)))
        loudness = loudness * jnp.repeat(heights, shape[dim] // shards_of).reshape([-1 if axis == dim else 1 for axis in range(len(shape))])
    return loudness


def scatter_about(stream_key, extent, width, most, pieces=(), kind=jnp.bfloat16):
    values = width * jax.random.normal(stream_key, extent, jnp.float32)
    if pieces:
        values = values * levels(stream_key, extent, pieces, -0.22, 0.18)
    return jnp.clip(values, -most, most).astype(kind)


def setup_inputs(seed: int = 0) -> dict:
    key_of = jax.random.split(jax.random.key(seed), 6)
    tracer = draw_tracer(jax.random.fold_in(key_of[5], 71), 0)
    kappa = jnp.clip(jnp.exp(math.log(0.24) - 1.3862944 * jax.random.uniform(key_of[1], (NX, NY), jnp.float32) ** levels(key_of[1], (NX, NY), ((0, 8), (1, 4)), -0.2, 0.2)), 0.06, 0.24)
    dkappa = scatter_about(key_of[2], (NX, NY), 1.0, 6.0, ((0, 8), (1, 4)), jnp.float32)
    precision_weight = draw_precision_weight(jax.random.fold_in(key_of[5], 71), 0)
    observed = touch_ends((jax.random.randint(key_of[4], (STEPS, NX // TILE, NY // TILE), 0, 2) < 1).astype(jnp.int32), jax.random.fold_in(key_of[4], 1), 0, 1)
    return dict(tracer=tracer, kappa=kappa, dkappa=dkappa, precision_weight=precision_weight, observed=observed)


shifts = ((1, 0), (-1, 0), (0, 1), (0, -1))


def pad_field(field, wide):
    wrapped = jnp.concatenate([field[..., -wide:, :], field, field[..., :wide, :]], axis=-2)
    config = [(0, 0)] * (field.ndim - 1) + [(wide, wide)]
    return jnp.pad(wrapped, config)


def neighbour(array, sx, sy):
    rows = array.shape[-2] - 2
    cols = array.shape[-1] - 2
    return array[..., 1 + sx:1 + sx + rows, 1 + sy:1 + sy + cols]


def tendency(coef, field):
    center = neighbour(field, 0, 0)
    coef_mid = neighbour(coef, 0, 0)
    total = jnp.zeros(center.shape, jnp.float32)
    for sx, sy in shifts:
        total = total + 0.5 * (coef_mid + neighbour(coef, sx, sy)) * (neighbour(field, sx, sy) - center)
    return total


def sensitivity(state, adjoint):
    state_mid = neighbour(state, 0, 0)
    adjoint_mid = neighbour(adjoint, 0, 0)
    total = jnp.zeros(state_mid.shape, jnp.float32)
    for sx, sy in shifts:
        total = total + (neighbour(state, sx, sy) - state_mid) * (neighbour(adjoint, sx, sy) - adjoint_mid)
    return -0.5 * jnp.sum(total, axis=tuple(range(total.ndim - 2)))


def regular(padded):
    center = neighbour(padded, 0, 0)
    total = 4.0 * center
    for sx, sy in shifts:
        total = total - neighbour(padded, sx, sy)
    return total


def spread_mask(observed):
    steps, tiles_x, tiles_y = observed.shape
    wide = jnp.broadcast_to(observed[:, :, None, :, None], (steps, tiles_x, TILE, tiles_y, TILE))
    return wide.reshape(steps, tiles_x * TILE, tiles_y * TILE).astype(jnp.float32)


def reference(tracer, kappa, dkappa, precision_weight, observed):
    kpad = pad_field(kappa, 1)
    dpad = pad_field(dkappa, 1)
    masks = spread_mask(observed)

    def layer(carry, field):
        grad, gram = carry
        base = field
        tangent = jnp.zeros_like(field)
        bases = []
        sources = []
        for step in range(STEPS):
            base_pad = pad_field(base, 1)
            tangent_pad = pad_field(tangent, 1)
            bases.append(base_pad)
            base_next = base + tendency(kpad, base_pad)
            tangent = tangent + tendency(kpad, tangent_pad) + tendency(dpad, base_pad)
            base = base_next
            masked = tangent * masks[step]
            gram = gram + jnp.einsum("cxy,dxy->cd", masked, tangent, precision=lax.Precision.HIGHEST)
            sources.append(masks[step] * jnp.einsum("cd,dxy->cxy", precision_weight, tangent, precision=lax.Precision.HIGHEST))
        adjoint = sources[-1]
        for step in reversed(range(STEPS)):
            adjoint_pad = pad_field(adjoint, 1)
            grad = grad + sensitivity(bases[step], adjoint_pad)
            if step > 0:
                adjoint = adjoint + tendency(kpad, adjoint_pad) + sources[step - 1]
        return (grad, gram), None

    start = (jnp.zeros((NX, NY), jnp.float32), jnp.zeros((CHANNELS, CHANNELS), jnp.float32))
    (grad, gram), unused = lax.scan(layer, start, tracer)
    hess_vec = grad + 0.5 * regular(dpad)
    cells = NX * NY
    curvature = jnp.sum(dkappa * hess_vec) / cells
    return hess_vec, gram / cells, curvature
```

```python
import functools

import jax
import jax.numpy as jnp
from jax import lax
from jax.experimental import pallas as pl
from jax.experimental.pallas import tpu as pltpu
from jax.sharding import PartitionSpec as P

STEPS = 4
HALO = 2 * STEPS
LANES = 128
MESH = pl.DeviceIdType.MESH
BF = jnp.bfloat16
F32 = jnp.float32


def east(v):
    return pltpu.roll(v, LANES - 1, v.ndim - 1)


def west(v):
    return pltpu.roll(v, 1, v.ndim - 1)


def sweep(lo, hi, n, body):
    count = (hi - lo) // n
    if count > 1:

        def one(i, carry):
            body(lo + i * n, n)
            return carry

        lax.fori_loop(0, count, one, 0)
    elif count == 1:
        body(lo, n)
    rest = (hi - lo) - count * n
    if rest:
        body(lo + count * n, rest)


def split(x):
    high = x.astype(BF).astype(F32)
    return high, x - high


def kernel(
    nx,
    ny,
    tracer_ref,
    kappa_ref,
    dkappa_ref,
    weight_ref,
    observed_ref,
    hess_ref,
    gram_ref,
    curv_ref,
    mb,
    mt,
    ma,
    mp,
    mc,
    mm,
    mge,
    mgs,
    sb,
    st,
    sa,
    sp,
    sc,
    sm,
    sge,
    sgs,
    edges,
    rim,
    cbuf,
    sums_y,
    sums_x,
    send_sem,
    recv_sem,
    ysend,
    yrecv,
    xsend,
    xrecv,
):
    gx = lax.axis_index("gx")
    gy = lax.axis_index("gy")
    north, south = lax.rem(gx + nx - 1, nx), lax.rem(gx + 1, nx)
    left, right = lax.rem(gy + ny - 1, ny), lax.rem(gy + 1, ny)

    barrier = pltpu.get_barrier_semaphore()
    friends = [(gx, lax.rem(gy + i, ny)) for i in range(1, ny)]
    friends += [(lax.rem(gx + i, nx), gy) for i in range(1, nx)]
    friends += [(north, left), (north, right), (south, left), (south, right)]
    for friend in friends:
        pl.semaphore_signal(barrier, inc=1, device_id=friend, device_id_type=MESH)

    lane = lax.broadcasted_iota(jnp.int32, (8, LANES), 1)
    own = jnp.swapaxes(tracer_ref[0], 0, 1)
    mb[0, 8:24] = own.reshape(16, 3, 8, LANES)
    cbuf[1, 3] = kappa_ref[0:8]
    cbuf[1, 4] = dkappa_ref[0:8]
    cbuf[1, 6] = kappa_ref[8:16]
    cbuf[1, 7] = dkappa_ref[8:16]
    tiles = observed_ref.shape[2]
    seen = observed_ref[:, 0, :].astype(F32)
    mask = jnp.zeros((STEPS, LANES), F32)
    spot = lax.broadcasted_iota(jnp.int32, (STEPS, LANES), 1) // (LANES // tiles)
    for i in range(tiles):
        mask = jnp.where(spot == i, seen[:, i : i + 1], mask)
    cbuf[1, 5] = jnp.concatenate([mask, jnp.zeros((8 - STEPS, LANES), F32)], axis=0)
    for half in range(2):
        packed = jnp.zeros((3, 8, LANES), F32)
        for s in range(8):
            row = mb[0, 8 + 8 * half + s]
            both = jnp.where(lane < 8, row, pltpu.roll(row, 16, 2))
            if s:
                both = pltpu.roll(both, 16 * s, 2)
            packed = jnp.where(lane // 16 == s, both, packed)
        edges[half] = packed

    pl.semaphore_wait(barrier, len(friends))

    plan = [
        (mb.at[0, 8:16], mb.at[0, 24:32], (north, gy)),
        (mb.at[0, 16:24], mb.at[0, 0:8], (south, gy)),
        (edges, rim.at[0, 1:3], (gx, right)),
        (edges, rim.at[1, 1:3], (gx, left)),
        (edges.at[0:1], rim.at[0, 3:4], (north, right)),
        (edges.at[0:1], rim.at[1, 3:4], (north, left)),
        (edges.at[1:2], rim.at[0, 0:1], (south, right)),
        (edges.at[1:2], rim.at[1, 0:1], (south, left)),
    ]
    mine = cbuf.at[1]
    plan += [
        (mine.at[3:6], cbuf.at[1, 8:11], (north, gy)),
        (mine.at[5:8], cbuf.at[1, 0:3], (south, gy)),
        (mine.at[3:8], cbuf.at[0, 3:8], (gx, right)),
        (mine.at[3:8], cbuf.at[2, 3:8], (gx, left)),
        (mine.at[3:6], cbuf.at[0, 8:11], (north, right)),
        (mine.at[3:6], cbuf.at[2, 8:11], (north, left)),
        (mine.at[5:8], cbuf.at[0, 0:3], (south, right)),
        (mine.at[5:8], cbuf.at[2, 0:3], (south, left)),
    ]
    copies = []
    for i, (src, dst, where) in enumerate(plan):
        copy = pltpu.make_async_remote_copy(
            src_ref=src,
            dst_ref=dst,
            send_sem=send_sem.at[i],
            recv_sem=recv_sem.at[i],
            device_id=where,
            device_id_type=MESH,
        )
        copy.start()
        copies.append(copy)

    weight_high, weight_low = split(weight_ref[...])
    weight_rows = jnp.concatenate([weight_high, weight_low], axis=0)
    weights = jnp.concatenate([weight_rows, weight_rows], axis=1).astype(BF)

    for copy in copies[8:]:
        copy.wait_recv()

    ok_left = jnp.where(gy > 0, 1.0, 0.0).astype(F32)
    ok_right = jnp.where(gy < ny - 1, 1.0, 0.0).astype(F32)
    one = jnp.ones((8, LANES), F32)
    inside_rim = jnp.where(lane % 16 < 8, ok_right * one, ok_left * one)
    domain_a = jnp.where(lane >= 112, inside_rim, one)
    domain = domain_a * pltpu.roll(domain_a, 64, 1)

    def sides(mid, rim_part):
        ax = mid.ndim - 1
        return jnp.where(
            lane < 16,
            mid,
            jnp.where(
                lane >= 112,
                rim_part,
                jnp.where(lane >= 96, pltpu.roll(mid, 112, ax), 0.0),
            ),
        )

    cmid = cbuf[1]
    crim = jnp.where(lane >= 120, cbuf[0], pltpu.roll(cbuf[2], 112, 2)) * inside_rim
    cside = sides(cmid, crim)

    def coefficients(kap, dk, out):
        rows = kap.shape[0]
        for index, field in ((0, kap), (2, dk)):
            face = 0.5 * (field + east(field))
            for r in range(1, rows - 1):
                out[index, r] = jnp.broadcast_to(face[r : r + 1], (8, LANES))
            face = 0.5 * (field[: rows - 1] + field[1:])
            for r in range(rows - 1):
                out[index + 1, r] = jnp.broadcast_to(face[r : r + 1], (8, LANES))

    def stack(source, picks):
        return jnp.concatenate([source[i] for i in picks], axis=0)

    k_main = stack(cmid, (1, 3, 6, 8))
    d_main = stack(cmid, (2, 4, 7, 9))
    k_all = stack(cside, (1, 3, 6, 8))
    d_all = stack(cside, (2, 4, 7, 9))
    k_side = k_all[:24] + pltpu.roll(k_all[8:], 64, 1)
    d_side = d_all[:24] + pltpu.roll(d_all[8:], 64, 1)
    coefficients(k_main, d_main, mc)
    coefficients(k_side, d_side, sc)

    side_mask = [
        cside[0] + pltpu.roll(cside[5], 64, 1),
        cside[5] + pltpu.roll(cside[5], 64, 1),
        cside[5] + pltpu.roll(cside[10], 64, 1),
    ]
    main_mask = [cmid[0], cmid[5], cmid[10]]
    for k in range(STEPS):
        for masks, out, cuts in (
            (main_mask, mm, (4, 8, 24, 28)),
            (side_mask, sm, (4, 8, 16, 20)),
        ):
            for part in range(3):
                wide = jnp.broadcast_to(masks[part][k : k + 1], (8, LANES))
                for r in range(cuts[part], cuts[part + 1]):
                    out[k, r] = wide

    def laplace(field, lo, hi):
        mid = field[lo:hi]
        return 4.0 * mid - east(mid) - west(mid) - field[lo - 1 : hi - 1] - field[lo + 1 : hi + 1]

    wide_lane = lax.broadcasted_iota(jnp.int32, (16, LANES), 1)

    def assemble(main, side):
        both = jnp.concatenate([side, pltpu.roll(side, 64, 1)], axis=0)
        return jnp.where(
            wide_lane < 8,
            both,
            jnp.where(wide_lane >= 120, pltpu.roll(both, 16, 1), main),
        )

    reg = assemble(laplace(d_main, 8, 24), laplace(d_side, 8, 16))
    energy = dkappa_ref[...] * reg
    energy = energy[0:8] + energy[8:16]

    for copy in copies[:8]:
        copy.wait_recv()

    for g in range(4):
        held = jnp.where(lane % 16 < 8, rim[1, g], rim[0, g]) * inside_rim
        for s in range(8):
            e = 8 * g + s
            turn = (112 - 16 * s) % LANES
            part = held if turn == 0 else pltpu.roll(held, turn, 2)
            cell = sides(mb[0, e], part)
            if e < 24:
                sb[0, e] = cell
            if e >= 8:
                sb[0, e - 8] = sb[0, e - 8] + pltpu.roll(cell, 64, 2)

    def forward(rows, base, tan, coef, dom, k):
        def body(r, n):
            b = base[k, pl.ds(r - 1, n + 2)]
            mid = b[1:-1]
            down = b[1:] - b[:-1]
            across = east(mid) - mid
            ke = coef[0, pl.ds(r, n)][:, None]
            ks = coef[1, pl.ds(r - 1, n + 1)][:, None]
            de = coef[2, pl.ds(r, n)][:, None]
            ds = coef[3, pl.ds(r - 1, n + 1)][:, None]

            def close(fs, fe):
                total = (fs[1:] - fs[:-1]) + (fe - west(fe))
                return total if dom is None else total * dom

            if k < STEPS - 1:
                base[k + 1, pl.ds(r, n)] = mid + close(ks * down, ke * across)
            fs = ds * down
            fe = de * across
            if k == 0:
                tan[0, pl.ds(r, n)] = close(fs, fe)
            else:
                t = tan[k - 1, pl.ds(r - 1, n + 2)]
                tmid = t[1:-1]
                fs = fs + ks * (t[1:] - t[:-1])
                fe = fe + ke * (east(tmid) - tmid)
                tan[k, pl.ds(r, n)] = tmid + close(fs, fe)

        sweep(k + 1, rows - k - 1, 4, body)

    for k in range(STEPS):
        forward(32, mb, mt, mc, None, k)
        forward(24, sb, st, sc, domain, k)

    main_cells = jnp.where((lane >= 8) & (lane < 120), 1.0, 0.0).astype(F32)
    side_cells = jnp.where(
        (lane < 8) | ((lane >= 104) & (lane < 112)) | ((lane >= 64) & (lane < 72)) | ((lane >= 40) & (lane < 48)),
        1.0,
        0.0,
    ).astype(F32)
    total = jnp.zeros((48, 48), F32)
    for tan, msk, cells, rows in ((mt, mm, main_cells, 16), (st, sm, side_cells, 8)):

        def gather(i, acc, tan=tan, msk=msk, cells=cells):
            r = 8 + 2 * i
            for k in range(STEPS):
                field = tan[k, pl.ds(r, 2)] * (msk[k, pl.ds(r, 2)] * cells)[:, None]
                high, low = split(field.reshape(2, 24, LANES))
                both = jnp.concatenate([high, low], axis=1)
                both = jnp.concatenate([both[0], both[1]], axis=1).astype(BF)
                acc = acc + lax.dot_general(
                    both, both, (((1,), (1,)), ((), ())), preferred_element_type=F32
                )
            return acc

        total = lax.fori_loop(0, rows // 2, gather, total)
    gram = total[:24, :24] + (total[:24, 24:] + total[24:, :24]) + total[24:, 24:]
    gram = jnp.concatenate([gram, jnp.zeros((24, LANES - 24), F32)], axis=1)

    sums_y[gy, 0:3] = gram.reshape(3, 8, LANES)
    sums_y[gy, 3] = energy
    ycopies = []
    for i in range(1, ny):
        copy = pltpu.make_async_remote_copy(
            src_ref=sums_y.at[gy],
            dst_ref=sums_y.at[gy],
            send_sem=ysend.at[i],
            recv_sem=yrecv.at[i],
            device_id=(gx, lax.rem(gy + i, ny)),
            device_id_type=MESH,
        )
        copy.start()
        ycopies.append(copy)

    def weigh(rows, base, out):
        def body(r, n):
            for k in range(STEPS):
                field = base[k, pl.ds(r, n)].reshape(n, 24, LANES)
                high, low = split(field)
                both = jnp.concatenate([high, low], axis=1)
                both = jnp.concatenate([both[i] for i in range(n)], axis=1).astype(BF)
                got = jnp.dot(weights, both, preferred_element_type=F32)
                got = got[:24] + got[24:]
                for i in range(n):
                    out[k, r + i] = got[:, i * LANES : (i + 1) * LANES].reshape(3, 8, LANES)

        sweep(7, rows - 7, 2, body)

    weigh(32, mb, mp)
    weigh(24, sb, sp)

    def backward(rows, tan, adj, coef, msk, dom, k):
        def last(r, n):
            adj[3, pl.ds(r, n)] = tan[3, pl.ds(r, n)] * msk[3, pl.ds(r, n)][:, None]

        def body(r, n):
            a = adj[k, pl.ds(r - 1, n + 2)]
            mid = a[1:-1]
            ke = coef[0, pl.ds(r, n)][:, None]
            ks = coef[1, pl.ds(r - 1, n + 1)][:, None]
            fs = ks * (a[1:] - a[:-1])
            fe = ke * (east(mid) - mid)
            change = (fs[1:] - fs[:-1]) + (fe - west(fe))
            if dom is not None:
                change = change * dom
            source = tan[k - 1, pl.ds(r, n)] * msk[k - 1, pl.ds(r, n)][:, None]
            adj[k - 1, pl.ds(r, n)] = mid + change + source

        if k == STEPS:
            sweep(4, rows - 4, 4, last)
        else:
            sweep(8 - k, rows - 8 + k, 4, body)

    for k in range(STEPS, 1, -1):
        backward(32, mt, ma, mc, mm, None, k)
        backward(24, st, sa, sc, sm, domain, k)

    for copy in ycopies:
        copy.wait_recv()
    part = sums_y[0]
    for i in range(1, ny):
        part = part + sums_y[i]
    sums_x[gx] = part
    xcopies = []
    for i in range(1, nx):
        copy = pltpu.make_async_remote_copy(
            src_ref=sums_x.at[gx],
            dst_ref=sums_x.at[gx],
            send_sem=xsend.at[i],
            recv_sem=xrecv.at[i],
            device_id=(lax.rem(gx + i, nx), gy),
            device_id_type=MESH,
        )
        copy.start()
        xcopies.append(copy)

    backward(32, mt, ma, mc, mm, None, 1)
    backward(24, st, sa, sc, sm, domain, 1)

    def products(rows, weighed, adj, ge, gs):
        def body(r, n):
            acc_e = jnp.zeros((n, 8, LANES), F32)
            acc_s = jnp.zeros((n, 8, LANES), F32)
            for k in range(STEPS):
                b = weighed[k, pl.ds(r, n + 1)]
                a = adj[k, pl.ds(r, n + 1)]
                acc_s = acc_s + jnp.sum((b[1:] - b[:-1]) * (a[1:] - a[:-1]), axis=1)
                b = b[:-1]
                a = a[:-1]
                acc_e = acc_e + jnp.sum((east(b) - b) * (east(a) - a), axis=1)
            ge[pl.ds(r, n)] = acc_e
            gs[pl.ds(r, n)] = acc_s

        sweep(7, rows - 8, 2, body)
        across = jnp.sum(ge[8 : rows - 8], axis=1)
        down = jnp.sum(gs[7 : rows - 8], axis=1)
        return -0.5 * (across + west(across) + down[1:] + down[:-1])

    main = products(32, mp, ma, mge, mgs)
    side = products(24, sp, sa, sge, sgs)
    hess_ref[...] = assemble(main, side) + 0.5 * reg

    for copy in xcopies:
        copy.wait_recv()
    part = sums_x[0]
    for i in range(1, nx):
        part = part + sums_x[i]
    scale = 1.0 / (16 * LANES * nx * ny)
    whole = part[0:3].reshape(24, LANES)[:, :24] * scale
    gram_ref[...] = whole
    quad = jnp.sum(jnp.sum(weight_ref[...] * whole, axis=1, keepdims=True), axis=0, keepdims=True)
    energy = jnp.sum(jnp.sum(part[3], axis=1, keepdims=True), axis=0, keepdims=True)
    curv_ref[...] = quad + (0.5 * scale) * energy

    for copy in copies + ycopies + xcopies:
        copy.wait_send()


def body(tracer, kappa, dkappa, precision_weight, observed):
    nx, ny = lax.axis_size("gx"), lax.axis_size("gy")

    def region(rows):
        field = pltpu.VMEM((STEPS, rows, 3, 8, LANES), F32)
        row = pltpu.VMEM((rows, 8, LANES), F32)
        return [field] * 4 + [pltpu.VMEM((4, rows, 8, LANES), F32)] * 2 + [row] * 2

    vmem = pl.BlockSpec(memory_space=pltpu.VMEM)
    hess, gram, curv = pl.pallas_call(
        functools.partial(kernel, nx, ny),
        out_shape=(
            jax.ShapeDtypeStruct(kappa.shape, F32),
            jax.ShapeDtypeStruct(precision_weight.shape, F32),
            jax.ShapeDtypeStruct((1, 1), F32),
        ),
        in_specs=[vmem] * 5,
        out_specs=(vmem,) * 3,
        scratch_shapes=region(32)
        + region(24)
        + [
            pltpu.VMEM((2, 3, 8, LANES), F32),
            pltpu.VMEM((2, 4, 3, 8, LANES), F32),
            pltpu.VMEM((3, 11, 8, LANES), F32),
            pltpu.VMEM((ny, 4, 8, LANES), F32),
            pltpu.VMEM((nx, 4, 8, LANES), F32),
            pltpu.SemaphoreType.DMA((16,)),
            pltpu.SemaphoreType.DMA((16,)),
            pltpu.SemaphoreType.DMA((ny,)),
            pltpu.SemaphoreType.DMA((ny,)),
            pltpu.SemaphoreType.DMA((nx,)),
            pltpu.SemaphoreType.DMA((nx,)),
        ],
        compiler_params=pltpu.CompilerParams(
            collective_id=0, has_side_effects=True, vmem_limit_bytes=40 * 1024 * 1024
        ),
    )(tracer, kappa, dkappa, precision_weight, observed)
    return hess, gram, curv.reshape(())


def solution(mesh):
    placed = (P(None, None, "gx", "gy"), P("gx", "gy"), P("gx", "gy"), P(), P(None, "gx", "gy"))
    return jax.shard_map(
        body, mesh=mesh, in_specs=placed, out_specs=(P("gx", "gy"), P(), P()), check_vma=False
    )
```

```python
import functools

import jax
import jax.numpy as jnp
from jax import lax
from jax.experimental import pallas as pl
from jax.experimental.pallas import tpu as pltpu
from jax.sharding import PartitionSpec as P

STEPS = 4
HALO = 2 * STEPS
LANES = 128
MESH = pl.DeviceIdType.MESH
BF = jnp.bfloat16
F32 = jnp.float32


def east(v):
    return pltpu.roll(v, LANES - 1, v.ndim - 1)


def west(v):
    return pltpu.roll(v, 1, v.ndim - 1)


def sweep(lo, hi, n, body):
    for r in range(lo, hi, n):
        body(r, min(n, hi - r))


def split(x):
    high = x.astype(BF).astype(F32)
    return high, x - high


def kernel(
    nx,
    ny,
    tracer_ref,
    kappa_ref,
    dkappa_ref,
    weight_ref,
    observed_ref,
    hess_ref,
    gram_ref,
    curv_ref,
    mb,
    mt,
    ma,
    mp,
    mc,
    mm,
    mge,
    mgs,
    sb,
    st,
    sa,
    sp,
    sc,
    sm,
    sge,
    sgs,
    edges,
    rim,
    cbuf,
    sums_y,
    sums_x,
    send_sem,
    recv_sem,
    ysend,
    yrecv,
    xsend,
    xrecv,
):
    gx = lax.axis_index("gx")
    gy = lax.axis_index("gy")
    north, south = lax.rem(gx + nx - 1, nx), lax.rem(gx + 1, nx)
    left, right = lax.rem(gy + ny - 1, ny), lax.rem(gy + 1, ny)

    barrier = pltpu.get_barrier_semaphore()
    friends = [(gx, lax.rem(gy + i, ny)) for i in range(1, ny)]
    friends += [(lax.rem(gx + i, nx), gy) for i in range(1, nx)]
    friends += [(north, left), (north, right), (south, left), (south, right)]
    for friend in friends:
        pl.semaphore_signal(barrier, inc=1, device_id=friend, device_id_type=MESH)

    lane = lax.broadcasted_iota(jnp.int32, (8, LANES), 1)
    own = jnp.swapaxes(tracer_ref[0], 0, 1)
    mb[0, 8:24] = own.reshape(16, 3, 8, LANES)
    cbuf[1, 3] = kappa_ref[0:8]
    cbuf[1, 4] = dkappa_ref[0:8]
    cbuf[1, 6] = kappa_ref[8:16]
    cbuf[1, 7] = dkappa_ref[8:16]
    tiles = observed_ref.shape[2]
    seen = observed_ref[:, 0, :].astype(F32)
    mask = jnp.zeros((STEPS, LANES), F32)
    spot = lax.broadcasted_iota(jnp.int32, (STEPS, LANES), 1) // (LANES // tiles)
    for i in range(tiles):
        mask = jnp.where(spot == i, seen[:, i : i + 1], mask)
    cbuf[1, 5] = jnp.concatenate([mask, jnp.zeros((8 - STEPS, LANES), F32)], axis=0)
    for half in range(2):
        packed = jnp.zeros((3, 8, LANES), F32)
        for s in range(8):
            row = mb[0, 8 + 8 * half + s]
            both = jnp.where(lane < 8, row, pltpu.roll(row, 16, 2))
            if s:
                both = pltpu.roll(both, 16 * s, 2)
            packed = jnp.where(lane // 16 == s, both, packed)
        edges[half] = packed

    pl.semaphore_wait(barrier, len(friends))

    plan = [
        (mb.at[0, 8:16], mb.at[0, 24:32], (north, gy)),
        (mb.at[0, 16:24], mb.at[0, 0:8], (south, gy)),
        (edges, rim.at[0, 1:3], (gx, right)),
        (edges, rim.at[1, 1:3], (gx, left)),
        (edges.at[0:1], rim.at[0, 3:4], (north, right)),
        (edges.at[0:1], rim.at[1, 3:4], (north, left)),
        (edges.at[1:2], rim.at[0, 0:1], (south, right)),
        (edges.at[1:2], rim.at[1, 0:1], (south, left)),
    ]
    mine = cbuf.at[1]
    plan += [
        (mine.at[3:6], cbuf.at[1, 8:11], (north, gy)),
        (mine.at[5:8], cbuf.at[1, 0:3], (south, gy)),
        (mine.at[3:8], cbuf.at[0, 3:8], (gx, right)),
        (mine.at[3:8], cbuf.at[2, 3:8], (gx, left)),
        (mine.at[3:6], cbuf.at[0, 8:11], (north, right)),
        (mine.at[3:6], cbuf.at[2, 8:11], (north, left)),
        (mine.at[5:8], cbuf.at[0, 0:3], (south, right)),
        (mine.at[5:8], cbuf.at[2, 0:3], (south, left)),
    ]
    copies = []
    for i, (src, dst, where) in enumerate(plan):
        copy = pltpu.make_async_remote_copy(
            src_ref=src,
            dst_ref=dst,
            send_sem=send_sem.at[i],
            recv_sem=recv_sem.at[i],
            device_id=where,
            device_id_type=MESH,
        )
        copy.start()
        copies.append(copy)

    weight_high, weight_low = split(weight_ref[...])
    weight_rows = jnp.concatenate([weight_high, weight_low], axis=0)
    weights = jnp.concatenate([weight_rows, weight_rows], axis=1).astype(BF)

    for copy in copies[8:]:
        copy.wait_recv()

    ok_left = jnp.where(gy > 0, 1.0, 0.0).astype(F32)
    ok_right = jnp.where(gy < ny - 1, 1.0, 0.0).astype(F32)
    one = jnp.ones((8, LANES), F32)
    inside_rim = jnp.where(lane % 16 < 8, ok_right * one, ok_left * one)
    domain_a = jnp.where(lane >= 112, inside_rim, one)
    domain = domain_a * pltpu.roll(domain_a, 64, 1)

    def sides(mid, rim_part):
        ax = mid.ndim - 1
        return jnp.where(
            lane < 16,
            mid,
            jnp.where(
                lane >= 112,
                rim_part,
                jnp.where(lane >= 96, pltpu.roll(mid, 112, ax), 0.0),
            ),
        )

    cmid = cbuf[1]
    crim = jnp.where(lane >= 120, cbuf[0], pltpu.roll(cbuf[2], 112, 2)) * inside_rim
    cside = sides(cmid, crim)

    def coefficients(kap, dk, out):
        rows = kap.shape[0]
        for index, field in ((0, kap), (2, dk)):
            face = 0.5 * (field + east(field))
            for r in range(1, rows - 1):
                out[index, r] = jnp.broadcast_to(face[r : r + 1], (8, LANES))
            face = 0.5 * (field[: rows - 1] + field[1:])
            for r in range(rows - 1):
                out[index + 1, r] = jnp.broadcast_to(face[r : r + 1], (8, LANES))

    def stack(source, picks):
        return jnp.concatenate([source[i] for i in picks], axis=0)

    k_main = stack(cmid, (1, 3, 6, 8))
    d_main = stack(cmid, (2, 4, 7, 9))
    k_all = stack(cside, (1, 3, 6, 8))
    d_all = stack(cside, (2, 4, 7, 9))
    k_side = k_all[:24] + pltpu.roll(k_all[8:], 64, 1)
    d_side = d_all[:24] + pltpu.roll(d_all[8:], 64, 1)
    coefficients(k_main, d_main, mc)
    coefficients(k_side, d_side, sc)

    side_mask = [
        cside[0] + pltpu.roll(cside[5], 64, 1),
        cside[5] + pltpu.roll(cside[5], 64, 1),
        cside[5] + pltpu.roll(cside[10], 64, 1),
    ]
    main_mask = [cmid[0], cmid[5], cmid[10]]
    for k in range(STEPS):
        for masks, out, cuts in (
            (main_mask, mm, (4, 8, 24, 28)),
            (side_mask, sm, (4, 8, 16, 20)),
        ):
            for part in range(3):
                wide = jnp.broadcast_to(masks[part][k : k + 1], (8, LANES))
                for r in range(cuts[part], cuts[part + 1]):
                    out[k, r] = wide

    def laplace(field, lo, hi):
        mid = field[lo:hi]
        return 4.0 * mid - east(mid) - west(mid) - field[lo - 1 : hi - 1] - field[lo + 1 : hi + 1]

    wide_lane = lax.broadcasted_iota(jnp.int32, (16, LANES), 1)

    def assemble(main, side):
        both = jnp.concatenate([side, pltpu.roll(side, 64, 1)], axis=0)
        return jnp.where(
            wide_lane < 8,
            both,
            jnp.where(wide_lane >= 120, pltpu.roll(both, 16, 1), main),
        )

    reg = assemble(laplace(d_main, 8, 24), laplace(d_side, 8, 16))
    energy = dkappa_ref[...] * reg
    energy = energy[0:8] + energy[8:16]

    for copy in copies[:8]:
        copy.wait_recv()

    for g in range(4):
        held = jnp.where(lane % 16 < 8, rim[1, g], rim[0, g]) * inside_rim
        for s in range(8):
            e = 8 * g + s
            turn = (112 - 16 * s) % LANES
            part = held if turn == 0 else pltpu.roll(held, turn, 2)
            cell = sides(mb[0, e], part)
            if e < 24:
                sb[0, e] = cell
            if e >= 8:
                sb[0, e - 8] = sb[0, e - 8] + pltpu.roll(cell, 64, 2)

    def forward(rows, base, tan, coef, dom, k):
        def body(r, n):
            b = base[k, pl.ds(r - 1, n + 2)]
            mid = b[1:-1]
            down = b[1:] - b[:-1]
            across = east(mid) - mid
            ke = coef[0, pl.ds(r, n)][:, None]
            ks = coef[1, pl.ds(r - 1, n + 1)][:, None]
            de = coef[2, pl.ds(r, n)][:, None]
            ds = coef[3, pl.ds(r - 1, n + 1)][:, None]

            def close(fs, fe):
                total = (fs[1:] - fs[:-1]) + (fe - west(fe))
                return total if dom is None else total * dom

            if k < STEPS - 1:
                base[k + 1, pl.ds(r, n)] = mid + close(ks * down, ke * across)
            fs = ds * down
            fe = de * across
            if k == 0:
                tan[0, pl.ds(r, n)] = close(fs, fe)
            else:
                t = tan[k - 1, pl.ds(r - 1, n + 2)]
                tmid = t[1:-1]
                fs = fs + ks * (t[1:] - t[:-1])
                fe = fe + ke * (east(tmid) - tmid)
                tan[k, pl.ds(r, n)] = tmid + close(fs, fe)

        sweep(k + 1, rows - k - 1, 4, body)

    for k in range(STEPS):
        forward(32, mb, mt, mc, None, k)
        forward(24, sb, st, sc, domain, k)

    main_cells = jnp.where((lane >= 8) & (lane < 120), 1.0, 0.0).astype(F32)
    side_cells = jnp.where(
        (lane < 8) | ((lane >= 104) & (lane < 112)) | ((lane >= 64) & (lane < 72)) | ((lane >= 40) & (lane < 48)),
        1.0,
        0.0,
    ).astype(F32)
    total = jnp.zeros((48, 48), F32)
    for tan, msk, cells, rows in ((mt, mm, main_cells, 16), (st, sm, side_cells, 8)):

        def gather(i, acc, tan=tan, msk=msk, cells=cells):
            r = 8 + 2 * i
            for k in range(STEPS):
                field = tan[k, pl.ds(r, 2)] * (msk[k, pl.ds(r, 2)] * cells)[:, None]
                high, low = split(field.reshape(2, 24, LANES))
                both = jnp.concatenate([high, low], axis=1)
                both = jnp.concatenate([both[0], both[1]], axis=1).astype(BF)
                acc = acc + lax.dot_general(
                    both, both, (((1,), (1,)), ((), ())), preferred_element_type=F32
                )
            return acc

        for i in range(rows // 2):
            total = gather(i, total)
    gram = total[:24, :24] + (total[:24, 24:] + total[24:, :24]) + total[24:, 24:]
    gram = jnp.concatenate([gram, jnp.zeros((24, LANES - 24), F32)], axis=1)

    sums_y[gy, 0:3] = gram.reshape(3, 8, LANES)
    sums_y[gy, 3] = energy
    ycopies = []
    for i in range(1, ny):
        copy = pltpu.make_async_remote_copy(
            src_ref=sums_y.at[gy],
            dst_ref=sums_y.at[gy],
            send_sem=ysend.at[i],
            recv_sem=yrecv.at[i],
            device_id=(gx, lax.rem(gy + i, ny)),
            device_id_type=MESH,
        )
        copy.start()
        ycopies.append(copy)

    def weigh(rows, base, out):
        def body(r, n):
            for k in range(STEPS):
                field = base[k, pl.ds(r, n)].reshape(n, 24, LANES)
                high, low = split(field)
                both = jnp.concatenate([high, low], axis=1)
                both = jnp.concatenate([both[i] for i in range(n)], axis=1).astype(BF)
                got = jnp.dot(weights, both, preferred_element_type=F32)
                got = got[:24] + got[24:]
                for i in range(n):
                    out[k, r + i] = got[:, i * LANES : (i + 1) * LANES].reshape(3, 8, LANES)

        sweep(7, rows - 7, 2, body)

    weigh(32, mb, mp)
    weigh(24, sb, sp)

    def backward(rows, tan, adj, coef, msk, dom, k):
        def last(r, n):
            adj[3, pl.ds(r, n)] = tan[3, pl.ds(r, n)] * msk[3, pl.ds(r, n)][:, None]

        def body(r, n):
            a = adj[k, pl.ds(r - 1, n + 2)]
            mid = a[1:-1]
            ke = coef[0, pl.ds(r, n)][:, None]
            ks = coef[1, pl.ds(r - 1, n + 1)][:, None]
            fs = ks * (a[1:] - a[:-1])
            fe = ke * (east(mid) - mid)
            change = (fs[1:] - fs[:-1]) + (fe - west(fe))
            if dom is not None:
                change = change * dom
            source = tan[k - 1, pl.ds(r, n)] * msk[k - 1, pl.ds(r, n)][:, None]
            adj[k - 1, pl.ds(r, n)] = mid + change + source

        if k == STEPS:
            sweep(4, rows - 4, 4, last)
        else:
            sweep(8 - k, rows - 8 + k, 4, body)

    for k in range(STEPS, 1, -1):
        backward(32, mt, ma, mc, mm, None, k)
        backward(24, st, sa, sc, sm, domain, k)

    for copy in ycopies:
        copy.wait_recv()
    part = sums_y[0]
    for i in range(1, ny):
        part = part + sums_y[i]
    sums_x[gx] = part
    xcopies = []
    for i in range(1, nx):
        copy = pltpu.make_async_remote_copy(
            src_ref=sums_x.at[gx],
            dst_ref=sums_x.at[gx],
            send_sem=xsend.at[i],
            recv_sem=xrecv.at[i],
            device_id=(lax.rem(gx + i, nx), gy),
            device_id_type=MESH,
        )
        copy.start()
        xcopies.append(copy)

    backward(32, mt, ma, mc, mm, None, 1)
    backward(24, st, sa, sc, sm, domain, 1)

    def products(rows, weighed, adj, ge, gs):
        def body(r, n):
            acc_e = jnp.zeros((n, 8, LANES), F32)
            acc_s = jnp.zeros((n, 8, LANES), F32)
            for k in range(STEPS):
                b = weighed[k, pl.ds(r, n + 1)]
                a = adj[k, pl.ds(r, n + 1)]
                acc_s = acc_s + jnp.sum((b[1:] - b[:-1]) * (a[1:] - a[:-1]), axis=1)
                b = b[:-1]
                a = a[:-1]
                acc_e = acc_e + jnp.sum((east(b) - b) * (east(a) - a), axis=1)
            ge[pl.ds(r, n)] = acc_e
            gs[pl.ds(r, n)] = acc_s

        sweep(7, rows - 8, 2, body)
        across = jnp.sum(ge[8 : rows - 8], axis=1)
        down = jnp.sum(gs[7 : rows - 8], axis=1)
        return -0.5 * (across + west(across) + down[1:] + down[:-1])

    main = products(32, mp, ma, mge, mgs)
    side = products(24, sp, sa, sge, sgs)
    hess_ref[...] = assemble(main, side) + 0.5 * reg

    for copy in xcopies:
        copy.wait_recv()
    part = sums_x[0]
    for i in range(1, nx):
        part = part + sums_x[i]
    scale = 1.0 / (16 * LANES * nx * ny)
    whole = part[0:3].reshape(24, LANES)[:, :24] * scale
    gram_ref[...] = whole
    quad = jnp.sum(jnp.sum(weight_ref[...] * whole, axis=1, keepdims=True), axis=0, keepdims=True)
    energy = jnp.sum(jnp.sum(part[3], axis=1, keepdims=True), axis=0, keepdims=True)
    curv_ref[...] = quad + (0.5 * scale) * energy

    for copy in copies + ycopies + xcopies:
        copy.wait_send()


def body(tracer, kappa, dkappa, precision_weight, observed):
    nx, ny = lax.axis_size("gx"), lax.axis_size("gy")

    def region(rows):
        field = pltpu.VMEM((STEPS, rows, 3, 8, LANES), F32)
        row = pltpu.VMEM((rows, 8, LANES), F32)
        return [field] * 4 + [pltpu.VMEM((4, rows, 8, LANES), F32)] * 2 + [row] * 2

    vmem = pl.BlockSpec(memory_space=pltpu.VMEM)
    hess, gram, curv = pl.pallas_call(
        functools.partial(kernel, nx, ny),
        out_shape=(
            jax.ShapeDtypeStruct(kappa.shape, F32),
            jax.ShapeDtypeStruct(precision_weight.shape, F32),
            jax.ShapeDtypeStruct((1, 1), F32),
        ),
        in_specs=[vmem] * 5,
        out_specs=(vmem,) * 3,
        scratch_shapes=region(32)
        + region(24)
        + [
            pltpu.VMEM((2, 3, 8, LANES), F32),
            pltpu.VMEM((2, 4, 3, 8, LANES), F32),
            pltpu.VMEM((3, 11, 8, LANES), F32),
            pltpu.VMEM((ny, 4, 8, LANES), F32),
            pltpu.VMEM((nx, 4, 8, LANES), F32),
            pltpu.SemaphoreType.DMA((16,)),
            pltpu.SemaphoreType.DMA((16,)),
            pltpu.SemaphoreType.DMA((ny,)),
            pltpu.SemaphoreType.DMA((ny,)),
            pltpu.SemaphoreType.DMA((nx,)),
            pltpu.SemaphoreType.DMA((nx,)),
        ],
        compiler_params=pltpu.CompilerParams(
            collective_id=0, has_side_effects=True, vmem_limit_bytes=40 * 1024 * 1024
        ),
    )(tracer, kappa, dkappa, precision_weight, observed)
    return hess, gram, curv.reshape(())


def solution(mesh):
    placed = (P(None, None, "gx", "gy"), P("gx", "gy"), P("gx", "gy"), P(), P(None, "gx", "gy"))
    return jax.shard_map(
        body, mesh=mesh, in_specs=placed, out_specs=(P("gx", "gy"), P(), P()), check_vma=False
    )
```

```python
import functools

import jax
import jax.numpy as jnp
from jax import lax
from jax.experimental import pallas as pl
from jax.experimental.pallas import tpu as pltpu
from jax.sharding import PartitionSpec as P

STEPS = 4
HALO = 2 * STEPS
LANES = 128
MESH = pl.DeviceIdType.MESH
BF = jnp.bfloat16
F32 = jnp.float32


def east(v):
    return pltpu.roll(v, LANES - 1, v.ndim - 1)


def west(v):
    return pltpu.roll(v, 1, v.ndim - 1)


def sweep(lo, hi, n, body):
    for r in range(lo, hi, n):
        body(r, min(n, hi - r))


def split(x):
    high = x.astype(BF).astype(F32)
    return high, x - high


def kernel(
    nx,
    ny,
    tracer_ref,
    kappa_ref,
    dkappa_ref,
    weight_ref,
    observed_ref,
    hess_ref,
    gram_ref,
    curv_ref,
    mb,
    mt,
    ma,
    mp,
    mc,
    mm,
    mge,
    mgs,
    sb,
    st,
    sa,
    sp,
    sc,
    sm,
    sge,
    sgs,
    edges,
    rim,
    cbuf,
    sums_y,
    sums_x,
    send_sem,
    recv_sem,
    ysend,
    yrecv,
    xsend,
    xrecv,
):
    gx = lax.axis_index("gx")
    gy = lax.axis_index("gy")
    north, south = lax.rem(gx + nx - 1, nx), lax.rem(gx + 1, nx)
    left, right = lax.rem(gy + ny - 1, ny), lax.rem(gy + 1, ny)

    barrier = pltpu.get_barrier_semaphore()
    friends = [(gx, lax.rem(gy + i, ny)) for i in range(1, ny)]
    friends += [(lax.rem(gx + i, nx), gy) for i in range(1, nx)]
    friends += [(north, left), (north, right), (south, left), (south, right)]
    for friend in friends:
        pl.semaphore_signal(barrier, inc=1, device_id=friend, device_id_type=MESH)

    lane = lax.broadcasted_iota(jnp.int32, (8, LANES), 1)
    own = jnp.swapaxes(tracer_ref[0], 0, 1)
    mb[0, 8:24] = own.reshape(16, 3, 8, LANES)
    cbuf[1, 3] = kappa_ref[0:8]
    cbuf[1, 4] = dkappa_ref[0:8]
    cbuf[1, 6] = kappa_ref[8:16]
    cbuf[1, 7] = dkappa_ref[8:16]
    tiles = observed_ref.shape[2]
    seen = observed_ref[:, 0, :].astype(F32)
    mask = jnp.zeros((STEPS, LANES), F32)
    spot = lax.broadcasted_iota(jnp.int32, (STEPS, LANES), 1) // (LANES // tiles)
    for i in range(tiles):
        mask = jnp.where(spot == i, seen[:, i : i + 1], mask)
    cbuf[1, 5] = jnp.concatenate([mask, jnp.zeros((8 - STEPS, LANES), F32)], axis=0)
    for half in range(2):
        packed = jnp.zeros((3, 8, LANES), F32)
        for s in range(8):
            row = mb[0, 8 + 8 * half + s]
            both = jnp.where(lane < 8, row, pltpu.roll(row, 16, 2))
            if s:
                both = pltpu.roll(both, 16 * s, 2)
            packed = jnp.where(lane // 16 == s, both, packed)
        edges[half] = packed

    pl.semaphore_wait(barrier, len(friends))

    plan = [
        (mb.at[0, 8:16], mb.at[0, 24:32], (north, gy)),
        (mb.at[0, 16:24], mb.at[0, 0:8], (south, gy)),
        (edges, rim.at[0, 1:3], (gx, right)),
        (edges, rim.at[1, 1:3], (gx, left)),
        (edges.at[0:1], rim.at[0, 3:4], (north, right)),
        (edges.at[0:1], rim.at[1, 3:4], (north, left)),
        (edges.at[1:2], rim.at[0, 0:1], (south, right)),
        (edges.at[1:2], rim.at[1, 0:1], (south, left)),
    ]
    mine = cbuf.at[1]
    plan += [
        (mine.at[3:6], cbuf.at[1, 8:11], (north, gy)),
        (mine.at[5:8], cbuf.at[1, 0:3], (south, gy)),
        (mine.at[3:8], cbuf.at[0, 3:8], (gx, right)),
        (mine.at[3:8], cbuf.at[2, 3:8], (gx, left)),
        (mine.at[3:6], cbuf.at[0, 8:11], (north, right)),
        (mine.at[3:6], cbuf.at[2, 8:11], (north, left)),
        (mine.at[5:8], cbuf.at[0, 0:3], (south, right)),
        (mine.at[5:8], cbuf.at[2, 0:3], (south, left)),
    ]
    copies = []
    for i, (src, dst, where) in enumerate(plan):
        copy = pltpu.make_async_remote_copy(
            src_ref=src,
            dst_ref=dst,
            send_sem=send_sem.at[i],
            recv_sem=recv_sem.at[i],
            device_id=where,
            device_id_type=MESH,
        )
        copy.start()
        copies.append(copy)

    weight_high, weight_low = split(weight_ref[...])
    weight_rows = jnp.concatenate([weight_high, weight_low], axis=0)
    weights = jnp.concatenate([weight_rows, weight_rows], axis=1).astype(BF)

    for copy in copies[8:]:
        copy.wait_recv()

    ok_left = jnp.where(gy > 0, 1.0, 0.0).astype(F32)
    ok_right = jnp.where(gy < ny - 1, 1.0, 0.0).astype(F32)
    one = jnp.ones((8, LANES), F32)
    inside_rim = jnp.where(lane % 16 < 8, ok_right * one, ok_left * one)
    domain_a = jnp.where(lane >= 112, inside_rim, one)
    domain = domain_a * pltpu.roll(domain_a, 64, 1)

    def sides(mid, rim_part):
        ax = mid.ndim - 1
        return jnp.where(
            lane < 16,
            mid,
            jnp.where(
                lane >= 112,
                rim_part,
                jnp.where(lane >= 96, pltpu.roll(mid, 112, ax), 0.0),
            ),
        )

    cmid = cbuf[1]
    crim = jnp.where(lane >= 120, cbuf[0], pltpu.roll(cbuf[2], 112, 2)) * inside_rim
    cside = sides(cmid, crim)

    def coefficients(kap, dk, out):
        rows = kap.shape[0]
        for index, field in ((0, kap), (2, dk)):
            face = 0.5 * (field + east(field))
            for r in range(1, rows - 1):
                out[index, r] = jnp.broadcast_to(face[r : r + 1], (8, LANES))
            face = 0.5 * (field[: rows - 1] + field[1:])
            for r in range(rows - 1):
                out[index + 1, r] = jnp.broadcast_to(face[r : r + 1], (8, LANES))

    def stack(source, picks):
        return jnp.concatenate([source[i] for i in picks], axis=0)

    k_main = stack(cmid, (1, 3, 6, 8))
    d_main = stack(cmid, (2, 4, 7, 9))
    k_all = stack(cside, (1, 3, 6, 8))
    d_all = stack(cside, (2, 4, 7, 9))
    k_side = k_all[:24] + pltpu.roll(k_all[8:], 64, 1)
    d_side = d_all[:24] + pltpu.roll(d_all[8:], 64, 1)
    coefficients(k_main, d_main, mc)
    coefficients(k_side, d_side, sc)

    side_mask = [
        cside[0] + pltpu.roll(cside[5], 64, 1),
        cside[5] + pltpu.roll(cside[5], 64, 1),
        cside[5] + pltpu.roll(cside[10], 64, 1),
    ]
    main_mask = [cmid[0], cmid[5], cmid[10]]
    for k in range(STEPS):
        for masks, out, cuts in (
            (main_mask, mm, (4, 8, 24, 28)),
            (side_mask, sm, (4, 8, 16, 20)),
        ):
            for part in range(3):
                wide = jnp.broadcast_to(masks[part][k : k + 1], (8, LANES))
                for r in range(cuts[part], cuts[part + 1]):
                    out[k, r] = wide

    def laplace(field, lo, hi):
        mid = field[lo:hi]
        return 4.0 * mid - east(mid) - west(mid) - field[lo - 1 : hi - 1] - field[lo + 1 : hi + 1]

    wide_lane = lax.broadcasted_iota(jnp.int32, (16, LANES), 1)

    def assemble(main, side):
        both = jnp.concatenate([side, pltpu.roll(side, 64, 1)], axis=0)
        return jnp.where(
            wide_lane < 8,
            both,
            jnp.where(wide_lane >= 120, pltpu.roll(both, 16, 1), main),
        )

    reg = assemble(laplace(d_main, 8, 24), laplace(d_side, 8, 16))
    energy = dkappa_ref[...] * reg
    energy = energy[0:8] + energy[8:16]

    def forward(lo, hi, base, tan, coef, dom, k):
        def body(r, n):
            b = base[k, pl.ds(r - 1, n + 2)]
            mid = b[1:-1]
            down = b[1:] - b[:-1]
            across = east(mid) - mid
            ke = coef[0, pl.ds(r, n)][:, None]
            ks = coef[1, pl.ds(r - 1, n + 1)][:, None]
            de = coef[2, pl.ds(r, n)][:, None]
            ds = coef[3, pl.ds(r - 1, n + 1)][:, None]

            def close(fs, fe):
                total = (fs[1:] - fs[:-1]) + (fe - west(fe))
                return total if dom is None else total * dom

            if k < STEPS - 1:
                base[k + 1, pl.ds(r, n)] = mid + close(ks * down, ke * across)
            fs = ds * down
            fe = de * across
            if k == 0:
                tan[0, pl.ds(r, n)] = close(fs, fe)
            else:
                t = tan[k - 1, pl.ds(r - 1, n + 2)]
                tmid = t[1:-1]
                fs = fs + ks * (t[1:] - t[:-1])
                fe = fe + ke * (east(tmid) - tmid)
                tan[k, pl.ds(r, n)] = tmid + close(fs, fe)

        sweep(lo, hi, 4, body)

    for k in range(STEPS):
        forward(9 + k, 23 - k, mb, mt, mc, None, k)

    for copy in copies[:8]:
        copy.wait_recv()

    for g in range(4):
        held = jnp.where(lane % 16 < 8, rim[1, g], rim[0, g]) * inside_rim
        for s in range(8):
            e = 8 * g + s
            turn = (112 - 16 * s) % LANES
            part = held if turn == 0 else pltpu.roll(held, turn, 2)
            cell = sides(mb[0, e], part)
            if e < 24:
                sb[0, e] = cell
            if e >= 8:
                sb[0, e - 8] = sb[0, e - 8] + pltpu.roll(cell, 64, 2)

    for k in range(STEPS):
        forward(k + 1, 9 + k, mb, mt, mc, None, k)
        forward(23 - k, 31 - k, mb, mt, mc, None, k)
        forward(k + 1, 23 - k, sb, st, sc, domain, k)

    main_cells = jnp.where((lane >= 8) & (lane < 120), 1.0, 0.0).astype(F32)
    side_cells = jnp.where(
        (lane < 8) | ((lane >= 104) & (lane < 112)) | ((lane >= 64) & (lane < 72)) | ((lane >= 40) & (lane < 48)),
        1.0,
        0.0,
    ).astype(F32)
    total = jnp.zeros((48, 48), F32)
    for tan, msk, cells, rows in ((mt, mm, main_cells, 16), (st, sm, side_cells, 8)):

        def gather(i, acc, tan=tan, msk=msk, cells=cells):
            r = 8 + 2 * i
            for k in range(STEPS):
                field = tan[k, pl.ds(r, 2)] * (msk[k, pl.ds(r, 2)] * cells)[:, None]
                high, low = split(field.reshape(2, 24, LANES))
                both = jnp.concatenate([high, low], axis=1)
                both = jnp.concatenate([both[0], both[1]], axis=1).astype(BF)
                acc = acc + lax.dot_general(
                    both, both, (((1,), (1,)), ((), ())), preferred_element_type=F32
                )
            return acc

        for i in range(rows // 2):
            total = gather(i, total)
    gram = total[:24, :24] + (total[:24, 24:] + total[24:, :24]) + total[24:, 24:]
    gram = jnp.concatenate([gram, jnp.zeros((24, LANES - 24), F32)], axis=1)

    sums_y[gy, 0:3] = gram.reshape(3, 8, LANES)
    sums_y[gy, 3] = energy
    ycopies = []
    for i in range(1, ny):
        copy = pltpu.make_async_remote_copy(
            src_ref=sums_y.at[gy],
            dst_ref=sums_y.at[gy],
            send_sem=ysend.at[i],
            recv_sem=yrecv.at[i],
            device_id=(gx, lax.rem(gy + i, ny)),
            device_id_type=MESH,
        )
        copy.start()
        ycopies.append(copy)

    def weigh(rows, base, out):
        def body(r, n):
            for k in range(STEPS):
                field = base[k, pl.ds(r, n)].reshape(n, 24, LANES)
                high, low = split(field)
                both = jnp.concatenate([high, low], axis=1)
                both = jnp.concatenate([both[i] for i in range(n)], axis=1).astype(BF)
                got = jnp.dot(weights, both, preferred_element_type=F32)
                got = got[:24] + got[24:]
                for i in range(n):
                    out[k, r + i] = got[:, i * LANES : (i + 1) * LANES].reshape(3, 8, LANES)

        sweep(7, rows - 7, 2, body)

    weigh(32, mb, mp)
    weigh(24, sb, sp)

    def backward(rows, tan, adj, coef, msk, dom, k):
        def last(r, n):
            adj[3, pl.ds(r, n)] = tan[3, pl.ds(r, n)] * msk[3, pl.ds(r, n)][:, None]

        def body(r, n):
            a = adj[k, pl.ds(r - 1, n + 2)]
            mid = a[1:-1]
            ke = coef[0, pl.ds(r, n)][:, None]
            ks = coef[1, pl.ds(r - 1, n + 1)][:, None]
            fs = ks * (a[1:] - a[:-1])
            fe = ke * (east(mid) - mid)
            change = (fs[1:] - fs[:-1]) + (fe - west(fe))
            if dom is not None:
                change = change * dom
            source = tan[k - 1, pl.ds(r, n)] * msk[k - 1, pl.ds(r, n)][:, None]
            adj[k - 1, pl.ds(r, n)] = mid + change + source

        if k == STEPS:
            sweep(4, rows - 4, 4, last)
        else:
            sweep(8 - k, rows - 8 + k, 4, body)

    for k in range(STEPS, 1, -1):
        backward(32, mt, ma, mc, mm, None, k)
        backward(24, st, sa, sc, sm, domain, k)

    for copy in ycopies:
        copy.wait_recv()
    part = sums_y[0]
    for i in range(1, ny):
        part = part + sums_y[i]
    sums_x[gx] = part
    xcopies = []
    for i in range(1, nx):
        copy = pltpu.make_async_remote_copy(
            src_ref=sums_x.at[gx],
            dst_ref=sums_x.at[gx],
            send_sem=xsend.at[i],
            recv_sem=xrecv.at[i],
            device_id=(lax.rem(gx + i, nx), gy),
            device_id_type=MESH,
        )
        copy.start()
        xcopies.append(copy)

    backward(32, mt, ma, mc, mm, None, 1)
    backward(24, st, sa, sc, sm, domain, 1)

    def products(rows, weighed, adj, ge, gs):
        def body(r, n):
            acc_e = jnp.zeros((n, 8, LANES), F32)
            acc_s = jnp.zeros((n, 8, LANES), F32)
            for k in range(STEPS):
                b = weighed[k, pl.ds(r, n + 1)]
                a = adj[k, pl.ds(r, n + 1)]
                acc_s = acc_s + jnp.sum((b[1:] - b[:-1]) * (a[1:] - a[:-1]), axis=1)
                b = b[:-1]
                a = a[:-1]
                acc_e = acc_e + jnp.sum((east(b) - b) * (east(a) - a), axis=1)
            ge[pl.ds(r, n)] = acc_e
            gs[pl.ds(r, n)] = acc_s

        sweep(7, rows - 8, 2, body)
        across = jnp.sum(ge[8 : rows - 8], axis=1)
        down = jnp.sum(gs[7 : rows - 8], axis=1)
        return -0.5 * (across + west(across) + down[1:] + down[:-1])

    main = products(32, mp, ma, mge, mgs)
    side = products(24, sp, sa, sge, sgs)
    hess_ref[...] = assemble(main, side) + 0.5 * reg

    for copy in xcopies:
        copy.wait_recv()
    part = sums_x[0]
    for i in range(1, nx):
        part = part + sums_x[i]
    scale = 1.0 / (16 * LANES * nx * ny)
    whole = part[0:3].reshape(24, LANES)[:, :24] * scale
    gram_ref[...] = whole
    quad = jnp.sum(jnp.sum(weight_ref[...] * whole, axis=1, keepdims=True), axis=0, keepdims=True)
    energy = jnp.sum(jnp.sum(part[3], axis=1, keepdims=True), axis=0, keepdims=True)
    curv_ref[...] = quad + (0.5 * scale) * energy

    for copy in copies + ycopies + xcopies:
        copy.wait_send()


def body(tracer, kappa, dkappa, precision_weight, observed):
    nx, ny = lax.axis_size("gx"), lax.axis_size("gy")

    def region(rows):
        field = pltpu.VMEM((STEPS, rows, 3, 8, LANES), F32)
        row = pltpu.VMEM((rows, 8, LANES), F32)
        return [field] * 4 + [pltpu.VMEM((4, rows, 8, LANES), F32)] * 2 + [row] * 2

    vmem = pl.BlockSpec(memory_space=pltpu.VMEM)
    hess, gram, curv = pl.pallas_call(
        functools.partial(kernel, nx, ny),
        out_shape=(
            jax.ShapeDtypeStruct(kappa.shape, F32),
            jax.ShapeDtypeStruct(precision_weight.shape, F32),
            jax.ShapeDtypeStruct((1, 1), F32),
        ),
        in_specs=[vmem] * 5,
        out_specs=(vmem,) * 3,
        scratch_shapes=region(32)
        + region(24)
        + [
            pltpu.VMEM((2, 3, 8, LANES), F32),
            pltpu.VMEM((2, 4, 3, 8, LANES), F32),
            pltpu.VMEM((3, 11, 8, LANES), F32),
            pltpu.VMEM((ny, 4, 8, LANES), F32),
            pltpu.VMEM((nx, 4, 8, LANES), F32),
            pltpu.SemaphoreType.DMA((16,)),
            pltpu.SemaphoreType.DMA((16,)),
            pltpu.SemaphoreType.DMA((ny,)),
            pltpu.SemaphoreType.DMA((ny,)),
            pltpu.SemaphoreType.DMA((nx,)),
            pltpu.SemaphoreType.DMA((nx,)),
        ],
        compiler_params=pltpu.CompilerParams(
            collective_id=0, has_side_effects=True, vmem_limit_bytes=40 * 1024 * 1024
        ),
    )(tracer, kappa, dkappa, precision_weight, observed)
    return hess, gram, curv.reshape(())


def solution(mesh):
    placed = (P(None, None, "gx", "gy"), P("gx", "gy"), P("gx", "gy"), P(), P(None, "gx", "gy"))
    return jax.shard_map(
        body, mesh=mesh, in_specs=placed, out_specs=(P("gx", "gy"), P(), P()), check_vma=False
    )
```
